32 devices in a mesh: gx: 4 (over z), gy: 4 (over y, core), gz: 2 (over x).
Axes of the slice: x: 2, y: 2, z: 4, core: 2. Of those that a mesh axis runs over, the one named last changes fastest.
Arguments:
- states: bfloat16 [192, 30720], P(None, ('gx', 'gy', 'gz')), may hold values from -16 to 16
- cell_matrices: bfloat16 [64, 512, 512], P(('gx', 'gy', 'gz')), as said below
- connectivity: int32 [64, 512], P(('gx', 'gy', 'gz')), may hold values from 0 to 959, as said below
- side_nodes: int32 [4, 3840], P(None, ('gx', 'gy', 'gz')), may hold values from 0 to 959, as said below
- top_nodes: int32 [2, 2048], P(None, ('gx', 'gy', 'gz')), may hold values from 0 to 959, as said below
- pot_index: int32 [30720], P(('gx', 'gy', 'gz')), may hold values from 0 to 63
- pot_table: float32 [64], replicated, may hold values from -1 to 1
Outputs:
- rotated: bfloat16 [192, 30720], P(None, ('gx', 'gy', 'gz'))
The draws below stay inside these ranges and needn't reach their ends.
Inputs may be any that keep to these rules, and one draw needn't show every extreme that they name: `connectivity`: slot numbers within one block; the nodes of one element take distinct slots. `side_nodes`: slot numbers within one block. `top_nodes`: slot numbers within one block. `cell_matrices`: each element's matrix is symmetric.
All inputs are finite; a program needn't handle non-finite values.
Results may differ from the reference program's by a relative error of at most 0.0067.
Values sent between devices are 32-bit elements; how exact they have to be, the bound alone decides.
No kernel may reach another device: no remote copies, remote signals or barrier semaphores. Data moves between devices by JAX's collectives and lax.ppermute only.
A program may use at most 64 MiB of HBM per device.

```python
import math
import jax
import jax.numpy as jnp
import numpy as np
from jax import lax

STATES = 192
EDGE = 8
CELLS_DEV = 2
TABLE = 64
NODES_CELL = 512
LOCAL = 960
SIDE = 120
TOP = 64
NODES = 30720
CELLS = 64
N_GX = 4
N_GY = 4
N_GZ = 2


def grid_slot(xpos, ypos, zpos):
    tall_nodes = 2 * EDGE - 1
    return (xpos * EDGE + ypos) * tall_nodes + zpos


def block_perms(key):
    blocks = CELLS // CELLS_DEV
    keys = jax.random.split(jax.random.fold_in(key, 7), blocks)
    return jax.vmap(lambda single: jax.random.permutation(single, LOCAL))(keys).astype(jnp.int32)


def cell_table():
    rows = []
    for elem_z in range(2):
        entries = []
        for along_a in range(EDGE):
            for along_b in range(EDGE):
                for along_c in range(EDGE):
                    entries.append(grid_slot(along_a, along_b, elem_z * (EDGE - 1) + along_c))
        rows.append(entries)
    return np.array(rows, dtype=np.int32)


def side_table():
    tall_nodes = 2 * EDGE - 1
    rows = []
    for level in (0, EDGE - 1):
        rows.append([grid_slot(level, ypos, zpos) for ypos in range(EDGE) for zpos in range(tall_nodes)])
    for level in (0, EDGE - 1):
        rows.append([grid_slot(xpos, level, zpos) for xpos in range(EDGE) for zpos in range(tall_nodes)])
    return np.array(rows, dtype=np.int32)


def top_table():
    tall_nodes = 2 * EDGE - 1
    rows = []
    for level in (0, tall_nodes - 1):
        rows.append([grid_slot(xpos, ypos, level) for xpos in range(EDGE) for ypos in range(EDGE)])
    return np.array(rows, dtype=np.int32)


def draw_connectivity(key, part):
    perms = block_perms(key)
    table = jnp.asarray(cell_table())
    picked = perms[:, table]
    return picked.reshape(CELLS, NODES_CELL).astype(jnp.int32)


def draw_side_nodes(key, part):
    perms = block_perms(key)
    table = jnp.asarray(side_table())
    picked = perms[:, table]
    return picked.transpose(1, 0, 2).reshape(4, -1).astype(jnp.int32)


def draw_top_nodes(key, part):
    perms = block_perms(key)
    table = jnp.asarray(top_table())
    picked = perms[:, table]
    return picked.transpose(1, 0, 2).reshape(2, -1).astype(jnp.int32)


def draw_cell_matrices(key, part):
    inner = jax.random.fold_in(key, 11)
    shape = (CELLS, NODES_CELL, NODES_CELL)
    raw = jax.random.normal(inner, shape, jnp.float32)
    sym = (raw + jnp.swapaxes(raw, 1, 2)) / jnp.sqrt(2.0)
    sym = jnp.clip(sym, -6.0, 6.0) / jnp.sqrt(float(NODES_CELL))
    return sym.astype(jnp.bfloat16)


def draw_states(key, part):
    keys = jax.random.split(jax.random.fold_in(key, 23), 5)
    shape = (STATES, NODES)
    shared_count = 4
    shared_weight = 0.35
    base = jnp.clip(jax.random.normal(keys[0], shape, jnp.float32), -4.0, 4.0)
    coeffs = shared_weight * jnp.clip(jax.random.normal(keys[1], (STATES, shared_count), jnp.float32), -3.0, 3.0)
    patterns = jnp.clip(jax.random.normal(keys[2], (shared_count, NODES), jnp.float32), -3.0, 3.0)
    shared = jnp.dot(coeffs, patterns, precision=lax.Precision.HIGHEST)
    column = jnp.exp(jax.random.uniform(keys[3], (1, NODES), jnp.float32, math.log(0.25), math.log(2.5)))
    row = jnp.exp(jax.random.uniform(keys[4], (STATES, 1), jnp.float32, math.log(0.7), math.log(1.4)))
    blocks = NODES // LOCAL
    place = (jnp.arange(NODES, dtype=jnp.int32) // LOCAL).astype(jnp.float32) / float(max(blocks - 1, 1))
    rise = jnp.exp(0.5 * math.log(3.0) * place)[None, :]
    values = row * column * rise * (base + shared)
    return jnp.clip(values, -16.0, 16.0).astype(jnp.bfloat16)


def with_ends(drawn, own_key, least, top_value):
    longest = drawn.shape.index(max(drawn.shape))
    spots = []
    for shift in (0, 1):
        where = [jax.random.randint(jax.random.fold_in(own_key, axis), (), 0, length) for axis, length in enumerate(drawn.shape)]
        where[longest] = (where[longest] + shift) % drawn.shape[longest]
        spots.append(tuple(where))
    return drawn.at[spots[0]].set(least).at[spots[1]].set(top_value)


def setup_inputs(seed: int = 0) -> dict:
    arg_keys = jax.random.split(jax.random.key(seed), 8)
    states = draw_states(jax.random.fold_in(arg_keys[7], 71), 0)
    cell_matrices = draw_cell_matrices(jax.random.fold_in(arg_keys[7], 71), 0)
    connectivity = draw_connectivity(jax.random.fold_in(arg_keys[7], 71), 0)
    side_nodes = draw_side_nodes(jax.random.fold_in(arg_keys[7], 71), 0)
    top_nodes = draw_top_nodes(jax.random.fold_in(arg_keys[7], 71), 0)
    pot_index = with_ends(jax.random.randint(arg_keys[5], (NODES,), 0, TABLE), jax.random.fold_in(arg_keys[5], 1), 0, TABLE - 1).astype(jnp.int32)
    pot_table = jnp.clip(jax.random.uniform(arg_keys[6], (TABLE,), jnp.float32, -1.0, 1.0), -1.0, 1.0)
    return {"states": states, "cell_matrices": cell_matrices, "connectivity": connectivity, "side_nodes": side_nodes, "top_nodes": top_nodes, "pot_index": pot_index, "pot_table": pot_table}


def cell_part(item):
    field, mats, conn = item
    cols = jnp.take(field, conn, axis=1).reshape(STATES, CELLS_DEV, NODES_CELL)
    prod = jnp.einsum('cij,scj->sci', mats.astype(jnp.float32), cols.astype(jnp.float32))
    zeros = jnp.zeros((STATES, LOCAL), jnp.float32)
    return zeros.at[:, conn].add(prod.reshape(STATES, CELLS_DEV * NODES_CELL))

def shift_axis(values, axis, upward):
    count = values.shape[axis]
    empty = jnp.zeros_like(lax.slice_in_dim(values, 0, 1, axis=axis))
    if upward:
        return jnp.concatenate([empty, lax.slice_in_dim(values, 0, count - 1, axis=axis)], axis=axis)
    return jnp.concatenate([lax.slice_in_dim(values, 1, count, axis=axis), empty], axis=axis)

def add_pair(block_sum, low_list, up_list, low_got, up_got):
    return block_sum.at[:, low_list].add(low_got).at[:, up_list].add(up_got)

def reference(states, cell_matrices, connectivity, side_nodes, top_nodes, pot_index, pot_table):
    blocks = N_GX * N_GY * N_GZ
    mats = cell_matrices.reshape(blocks, CELLS_DEV, NODES_CELL, NODES_CELL)
    conn = connectivity.reshape(blocks, CELLS_DEV * NODES_CELL).astype(jnp.int32)
    sides = side_nodes.reshape(4, blocks, SIDE).transpose(1, 0, 2).astype(jnp.int32)
    tops = top_nodes.reshape(2, blocks, TOP).transpose(1, 0, 2).astype(jnp.int32)
    face_lists = [(sides[:, 0], sides[:, 1]), (sides[:, 2], sides[:, 3]), (tops[:, 0], tops[:, 1])]
    potential = pot_table[pot_index.astype(jnp.int32)].reshape(blocks, 1, LOCAL)
    picker = jax.vmap(lambda values, index: values[:, index])

    def apply(field):
        rounded = field.astype(jnp.bfloat16)
        cellsum = lax.map(cell_part, (rounded, mats, conn))
        total = cellsum
        for direction in range(3):
            low_list, up_list = face_lists[direction]
            count = low_list.shape[1]
            low_vals = picker(cellsum, low_list).reshape(N_GX, N_GY, N_GZ, STATES, count)
            up_vals = picker(cellsum, up_list).reshape(N_GX, N_GY, N_GZ, STATES, count)
            low_got = shift_axis(up_vals, direction, True).reshape(blocks, STATES, count)
            up_got = shift_axis(low_vals, direction, False).reshape(blocks, STATES, count)
            total = jax.vmap(add_pair)(total, low_list, up_list, low_got, up_got)
        return total + potential * field
    start = states.astype(jnp.float32).reshape(STATES, blocks, LOCAL).transpose(1, 0, 2)
    first = (apply(start) - 0.5 * start) / 3.0
    second = 2.0 * (apply(first) - 0.5 * first) / 3.0 - start
    filtered = second.astype(jnp.bfloat16).transpose(1, 0, 2).reshape(STATES, NODES)
    correlation = jnp.dot(filtered.astype(jnp.float32), filtered.T.astype(jnp.float32), preferred_element_type=jnp.float32) / NODES
    lower = jnp.linalg.cholesky(correlation)
    inverse = jax.scipy.linalg.solve_triangular(lower, jnp.eye(STATES, dtype=jnp.float32), lower=True)
    inverse = inverse.astype(jnp.bfloat16)
    return jnp.dot(inverse.astype(jnp.float32), filtered.astype(jnp.float32), preferred_element_type=jnp.float32).astype(jnp.bfloat16)
```

```python
import functools

import jax
import jax.numpy as jnp
from jax import lax
from jax.experimental import pallas as pl
from jax.experimental.pallas import tpu as pltpu
from jax.sharding import PartitionSpec as P

LANES = 128
SUBS = 8
BLOCK = 32
VMEM = 40 * 2**20
F32 = jnp.float32
BF16 = jnp.bfloat16
AXES = ("gx", "gy", "gz")
NN = (((1,), (0,)), ((), ()))
NT = (((1,), (1,)), ((), ()))


def mm(lhs, rhs, dims=NN):
    return lax.dot_general(lhs, rhs, dims, preferred_element_type=F32)


def mm32(lhs, rhs, dims=NN):
    return lax.dot_general(
        lhs, rhs, dims, precision=lax.Precision.HIGHEST, preferred_element_type=F32
    )


def split(value):
    high = value.astype(BF16)
    low = (value - high.astype(F32)).astype(BF16)
    return jnp.concatenate([high, low], axis=0)


def mm_split(value, rhs, dims=NN):
    both = mm(split(value), rhs, dims)
    rows = value.shape[0]
    return both[:rows] + both[rows:]


def padded(count):
    return -(-count // LANES) * LANES


class Plan:
    def __init__(self, mesh_sizes, side, top):
        self.lists = []
        place = 0
        for axis in range(3):
            count = side if axis < 2 else top
            wide = padded(count)
            for phase in range(2):
                if phase == 0 or mesh_sizes[axis] > 2:
                    self.lists.append((axis, phase, count, place, wide))
                    place += wide
        self.total = place


def one_hot(indices, rows):
    shape = (rows, indices.shape[1])
    return jnp.where(lax.broadcasted_iota(jnp.int32, shape, 0) == indices, 1.0, 0.0).astype(BF16)


def face_matrix(plan, parities, sides_ref, tops_ref, faces_ref):
    slots = faces_ref.shape[0]
    for axis, phase, count, place, wide in plan.lists:
        ref, row = (sides_ref, 2 * axis) if axis < 2 else (tops_ref, 0)
        lower, upper = ref[row : row + 1, :], ref[row + 1 : row + 2, :]
        take_lower = parities[axis] != phase
        chosen = jnp.where(take_lower, lower, upper)
        if wide > count:
            chosen = jnp.concatenate([chosen, jnp.full((1, wide - count), -1, jnp.int32)], axis=1)
        faces_ref[:, place : place + wide] = one_hot(chosen, slots)


def shifted_potential(index_ref, table_ref):
    levels = table_ref.shape[1]
    picks = one_hot(index_ref[...], levels)
    table = table_ref[...]
    first = table.astype(BF16)
    rest = table - first.astype(F32)
    second = rest.astype(BF16)
    third = (rest - second.astype(F32)).astype(BF16)
    parts = mm(jnp.concatenate([first, second, third, first, first, first, first, first], 0), picks)
    return parts[0:1] + parts[1:2] + parts[2:3] - 0.5


def cell_sum(rounded, mats_ref, conn_ref):
    slots = rounded.shape[1]
    total = None
    for cell in range(mats_ref.shape[0]):
        spots = one_hot(conn_ref[cell : cell + 1, :], slots)
        nodes = mm(rounded, spots).astype(BF16)
        prod = mm(nodes, mats_ref[cell], NT)
        part = mm_split(prod, spots, NT)
        total = part if total is None else total + part
    return total


def parity_of_axes():
    return [lax.rem(lax.axis_index(axis), 2) for axis in AXES]


def send_faces(plan, cellsum, faces_ref, send_refs):
    out = mm_split(cellsum, faces_ref[...])
    for (_, _, count, place, _), ref in zip(plan.lists, send_refs):
        ref[...] = out[:, place : place + ref.shape[1]]


def got_faces(plan, recv_refs, faces_ref, got_ref):
    for (_, _, _, place, wide), ref in zip(plan.lists, recv_refs):
        got = ref[...]
        if got.shape[1] < wide:
            got_ref[:, place : place + wide] = jnp.zeros((got.shape[0], wide), F32)
        got_ref[:, place : place + got.shape[1]] = got
    return mm_split(got_ref[...], faces_ref[...], NT)


def first_kernel(plan, par_ref, states_ref, mats_ref, conn_ref, sides_ref, tops_ref, index_ref, table_ref, part_ref, *rest):
    send_refs, faces_ref = rest[:-1], rest[-1]
    face_matrix(plan, [par_ref[axis] for axis in range(3)], sides_ref, tops_ref, faces_ref)
    states = states_ref[...]
    cellsum = cell_sum(states, mats_ref, conn_ref)
    send_faces(plan, cellsum, faces_ref, send_refs)
    part_ref[...] = cellsum + shifted_potential(index_ref, table_ref) * states.astype(F32)


def second_kernel(plan, par_ref, states_ref, mats_ref, conn_ref, sides_ref, tops_ref, index_ref, table_ref, part_ref, *rest):
    count = len(plan.lists)
    recv_refs, out_ref, send_refs = rest[:count], rest[count], rest[count + 1 : 2 * count + 1]
    faces_ref, got_ref = rest[2 * count + 1 :]
    face_matrix(plan, [par_ref[axis] for axis in range(3)], sides_ref, tops_ref, faces_ref)
    first = (part_ref[...] + got_faces(plan, recv_refs, faces_ref, got_ref)) / 3.0
    cellsum = cell_sum(first.astype(BF16), mats_ref, conn_ref)
    send_faces(plan, cellsum, faces_ref, send_refs)
    applied = cellsum + shifted_potential(index_ref, table_ref) * first
    out_ref[...] = 2.0 * applied / 3.0 - states_ref[...].astype(F32)


def third_kernel(plan, par_ref, sides_ref, tops_ref, part_ref, *rest):
    count = len(plan.lists)
    recv_refs, filtered_ref, mine_ref, other_ref = rest[:count], rest[count], rest[count + 1], rest[count + 2]
    faces_ref, got_ref, gram_ref = rest[count + 3 :]
    face_matrix(plan, [par_ref[axis] for axis in range(3)], sides_ref, tops_ref, faces_ref)
    got = got_faces(plan, recv_refs, faces_ref, got_ref)
    filtered = (part_ref[...] + got * (2.0 / 3.0)).astype(BF16)
    filtered_ref[...] = filtered
    gram = mm(filtered, filtered, NT)
    third = gram.shape[0] // 3
    gram_ref[...] = gram[:, : 2 * third]
    gram_ref[:third, third:] = gram[2 * third :, 2 * third :]
    half = mine_ref.shape[0]
    core = par_ref[1]
    mine_ref[...] = gram_ref[pl.ds(pl.multiple_of(core * half, SUBS), half), :]
    other_ref[...] = gram_ref[pl.ds(pl.multiple_of((1 - core) * half, SUBS), half), :]


def invert_block(mat_ref, lead, lane0):
    tiles = BLOCK // SUBS
    shape = (SUBS, LANES)
    sub = lax.broadcasted_iota(jnp.int32, shape, 0)
    lane = lax.broadcasted_iota(jnp.int32, shape, 1)
    shift = lead - lane0

    def row(value, index):
        return jnp.broadcast_to(value[index : index + 1, :], shape)

    wide = min(LANES, mat_ref.shape[1] - lane0)
    rows = []
    for tile in range(tiles):
        loaded = mat_ref[lead + SUBS * tile : lead + SUBS * (tile + 1), lane0 : lane0 + wide]
        rows.append(loaded)
    cols = [
        [
            jnp.broadcast_to(rows[tile][:, shift + col : shift + col + 1], shape) if tile >= col // SUBS else None
            for tile in range(tiles)
        ]
        for col in range(BLOCK)
    ]
    inverse = [jnp.where(sub + (SUBS * tile + shift) == lane, 1.0, 0.0).astype(F32) for tile in range(tiles)]
    for col in range(BLOCK):
        own, at = divmod(col, SUBS)
        root = lax.rsqrt(row(cols[col][own], at))
        scaled = [cols[col][tile] * root if tile >= own else None for tile in range(tiles)]
        for later in range(col + 1, BLOCK):
            factor = row(scaled[later // SUBS], later % SUBS)
            for tile in range(later // SUBS, tiles):
                cols[later][tile] = cols[later][tile] - scaled[tile] * factor
        pivot_row = row(inverse[own], at) * root
        for tile in range(own, tiles):
            if tile == own:
                below = jnp.where(sub > at, scaled[tile], 0.0)
                inverse[tile] = jnp.where(sub == at, pivot_row, inverse[tile] - below * pivot_row)
            else:
                inverse[tile] = inverse[tile] - scaled[tile] * pivot_row
    return jnp.concatenate(inverse, axis=0)[:, :wide]


def rotate_kernel(total_slots, par_ref, mine_ref, other_ref, filtered_ref, out_ref, packed_ref, mat_ref, acc_ref, inv_ref):
    width = mat_ref.shape[0]
    half = mine_ref.shape[0]
    third = width // 3
    core = par_ref[1]
    packed_ref[pl.ds(pl.multiple_of(core * half, SUBS), half), :] = mine_ref[...]
    packed_ref[pl.ds(pl.multiple_of((1 - core) * half, SUBS), half), :] = other_ref[...]
    packed = packed_ref[...] / total_slots
    mat_ref[:, : 2 * third] = packed
    mat_ref[: 2 * third, 2 * third :] = jnp.zeros((2 * third, third), F32)
    mat_ref[2 * third :, 2 * third :] = packed[:third, third:]
    full = (width, width)
    row = lax.broadcasted_iota(jnp.int32, full, 0)
    col = lax.broadcasted_iota(jnp.int32, full, 1)
    eye = row == col
    mat = mat_ref[...]
    diagonal = jnp.where(eye, mat, 0.0)
    scale_col = lax.rsqrt(jnp.sum(diagonal, axis=1, keepdims=True))
    scale_row = lax.rsqrt(jnp.sum(diagonal, axis=0, keepdims=True))
    mat_ref[...] = jnp.where(row >= col - col % BLOCK, mat * scale_col * scale_row, 0.0)
    acc_ref[...] = jnp.where(eye, 1.0, 0.0)
    for lead in range(0, width, BLOCK):
        lane0 = lead // LANES * LANES
        wide = min(LANES, width - lane0)
        block = invert_block(mat_ref, lead, lane0)
        rows_inv = mm32(block, acc_ref[lane0 : lane0 + wide, :])
        inv_ref[lead : lead + BLOCK, :] = (rows_inv * scale_row).astype(BF16)
        after = lead + BLOCK
        if after < width:
            lower = mm32(mat_ref[after:, lane0 : lane0 + wide], block, NT)
            whole = jnp.concatenate([jnp.zeros((after, BLOCK), F32), lower], axis=0)
            mat_ref[after:, :] = mat_ref[after:, :] - mm32(lower, whole, NT)
            acc_ref[after:, :] = acc_ref[after:, :] - mm32(lower, rows_inv)
    out_ref[...] = mm(inv_ref[...], filtered_ref[...]).astype(BF16)


def call(kernel, outs, scratch, *args):
    smem = pl.BlockSpec(memory_space=pltpu.SMEM)
    vmem = pl.BlockSpec(memory_space=pltpu.VMEM)
    return pl.pallas_call(
        kernel,
        out_shape=outs,
        in_specs=[smem] + [vmem] * (len(args) - 1),
        out_specs=jax.tree.map(lambda _: vmem, outs),
        scratch_shapes=scratch,
        compiler_params=pltpu.CompilerParams(vmem_limit_bytes=VMEM),
    )(*args)


def pairs_of(size, phase):
    ups = [(i, i + 1) for i in range(phase, size - 1, 2)]
    return ups + [(j, i) for i, j in ups]


def swap_steps():
    steps = []
    for axis, least in (("gy", 2), ("gz", 1), ("gx", 1)):
        size = lax.axis_size(axis)
        reach = least
        while reach < size:
            steps.append((axis, [(i, i ^ reach) for i in range(size)]))
            reach *= 2
    return steps


def on_device(states, cell_matrices, connectivity, side_nodes, top_nodes, pot_index, pot_table):
    width, slots = states.shape
    sizes = [lax.axis_size(axis) for axis in AXES]
    plan = Plan(sizes, side_nodes.shape[1], top_nodes.shape[1])
    parities = jnp.stack(parity_of_axes()).astype(jnp.int32)
    index = pot_index.reshape(1, slots)
    table = pot_table.reshape(1, -1)
    field = jax.ShapeDtypeStruct((width, slots), F32)
    sends = [
        jax.ShapeDtypeStruct((width, wide if count > LANES // 2 else count), F32)
        for _, _, count, _, wide in plan.lists
    ]
    faces = pltpu.VMEM((slots, plan.total), BF16)
    got = pltpu.VMEM((width, plan.total), F32)

    def swap(values):
        return [
            lax.ppermute(value, AXES[axis], pairs_of(sizes[axis], phase))
            for value, (axis, phase, _, _, _) in zip(values, plan.lists)
        ]

    geometry = (cell_matrices, connectivity, side_nodes, top_nodes, index, table)
    part, *sent = call(
        functools.partial(first_kernel, plan), [field, *sends], [faces], parities, states, *geometry
    )
    part, *sent = call(
        functools.partial(second_kernel, plan),
        [field, *sends],
        [faces, got],
        parities,
        states,
        *geometry,
        part,
        *swap(sent),
    )
    third = width // 3
    half = jax.ShapeDtypeStruct((width // 2, 2 * third), F32)
    filtered, mine, other = call(
        functools.partial(third_kernel, plan),
        [jax.ShapeDtypeStruct((width, slots), BF16), half, half],
        [faces, got, pltpu.VMEM((width, 2 * third), F32)],
        parities,
        side_nodes,
        top_nodes,
        part,
        *swap(sent),
    )
    mates = pairs_of(sizes[1], 0)
    mine = mine + lax.ppermute(other, "gy", mates)
    for axis, pairs in swap_steps():
        mine = mine + lax.ppermute(mine, axis, pairs)
    other = lax.ppermute(mine, "gy", mates)
    total_slots = slots * sizes[0] * sizes[1] * sizes[2]
    square = pltpu.VMEM((width, width), F32)
    return call(
        functools.partial(rotate_kernel, total_slots),
        jax.ShapeDtypeStruct((width, slots), BF16),
        [pltpu.VMEM((width, 2 * third), F32), square, square, pltpu.VMEM((width, width), BF16)],
        parities,
        mine,
        other,
        filtered,
    )


def solution(mesh):
    in_specs = (
        P(None, AXES),
        P(AXES, None, None),
        P(AXES, None),
        P(None, AXES),
        P(None, AXES),
        P(AXES),
        P(),
    )
    return jax.shard_map(
        on_device, mesh=mesh, in_specs=in_specs, out_specs=P(None, AXES), check_vma=False
    )
```

```python
import functools

import jax
import jax.numpy as jnp
from jax import lax
from jax.experimental import pallas as pl
from jax.experimental.pallas import tpu as pltpu
from jax.sharding import PartitionSpec as P

LANES = 128
SUBS = 8
BLOCK = 32
VMEM = 40 * 2**20
WHOLE_VMEM = 56 * 2**20
F32 = jnp.float32
BF16 = jnp.bfloat16
AXES = ("gx", "gy", "gz")
NN = (((1,), (0,)), ((), ()))
NT = (((1,), (1,)), ((), ()))


def mm(lhs, rhs, dims=NN):
    return lax.dot_general(lhs, rhs, dims, preferred_element_type=F32)


def mm32(lhs, rhs, dims=NN):
    return lax.dot_general(
        lhs, rhs, dims, precision=lax.Precision.HIGHEST, preferred_element_type=F32
    )


def split(value):
    high = value.astype(BF16)
    low = (value - high.astype(F32)).astype(BF16)
    return jnp.concatenate([high, low], axis=0)


def mm_split(value, rhs, dims=NN):
    both = mm(split(value), rhs, dims)
    rows = value.shape[0]
    return both[:rows] + both[rows:]


def padded(count):
    return -(-count // LANES) * LANES


class Plan:
    def __init__(self, mesh_sizes, side, top):
        self.lists = []
        self.total = 0
        for axis, phase in ((0, 0), (0, 1), (1, 1), (2, 0), (2, 1), (1, 0)):
            if phase == 0 or mesh_sizes[axis] > 2:
                count = side if axis < 2 else top
                self.lists.append((axis, phase, count, self.total))
                self.total += padded(count)

    def sent_shape(self, count, width):
        if 2 * count <= LANES and width % (2 * SUBS) == 0:
            return (width // 2, LANES)
        return (width, padded(count))


def one_hot(indices, rows):
    shape = (rows, indices.shape[1])
    return jnp.where(lax.broadcasted_iota(jnp.int32, shape, 0) == indices, 1.0, 0.0).astype(BF16)


def face_slots(plan, sides, tops):
    parts = []
    parities = [lax.rem(lax.axis_index(axis), 2) for axis in AXES]
    for axis, phase, count, _ in plan.lists:
        ref, row = (sides, 2 * axis) if axis < 2 else (tops, 0)
        lower, upper = ref[row : row + 1, :], ref[row + 1 : row + 2, :]
        parts.append(jnp.where(parities[axis] != phase, lower, upper))
        if padded(count) > count:
            parts.append(jnp.full((1, padded(count) - count), -1, jnp.int32))
    return jnp.concatenate(parts, axis=1)


def shifted_potential(index_ref, table_ref):
    levels = table_ref.shape[1]
    picks = one_hot(index_ref[...], levels)
    table = table_ref[...]
    first = table.astype(BF16)
    rest = table - first.astype(F32)
    second = rest.astype(BF16)
    third = (rest - second.astype(F32)).astype(BF16)
    parts = mm(jnp.concatenate([first, second, third, first, first, first, first, first], 0), picks)
    return parts[0:1] + parts[1:2] + parts[2:3] - 0.5


def element_products(rounded, mats_ref, spots_ref, prods_ref):
    for cell in range(mats_ref.shape[0]):
        nodes = mm(rounded, spots_ref[cell]).astype(BF16)
        prods_ref[cell] = split(mm(nodes, mats_ref[cell]))


def joined(both):
    rows = both.shape[0] // 2
    return both[:rows] + both[rows:]


def over_cells(prods_ref, other_ref, dims):
    total = None
    for cell in range(prods_ref.shape[0]):
        part = mm(prods_ref[cell], other_ref[cell], dims)
        total = part if total is None else total + part
    return joined(total)


def send_faces(plan, prods_ref, match_ref, send_refs):
    out = over_cells(prods_ref, match_ref, NN)
    for (_, _, count, place), ref in zip(plan.lists, send_refs):
        rows = ref.shape[0]
        if rows < out.shape[0]:
            ref[:, :count] = out[:rows, place : place + count]
            ref[:, LANES // 2 : LANES // 2 + count] = out[rows:, place : place + count]
        else:
            ref[...] = out[:, place : place + ref.shape[1]]


def got_faces(plan, recv_refs, faces_ref, got_ref):
    width = got_ref.shape[0]
    for (_, _, count, place), ref in zip(plan.lists, recv_refs):
        rows = ref.shape[0]
        wide = padded(count)
        if rows < width:
            got_ref[:, place : place + wide] = jnp.zeros((width, wide), F32)
            got_ref[:rows, place : place + count] = ref[:, :count]
            got_ref[rows:, place : place + count] = ref[:, LANES // 2 : LANES // 2 + count]
        else:
            got_ref[:, place : place + wide] = ref[...]
    return mm_split(got_ref[...], faces_ref[...], NT)


def matches(conn, columns):
    cells, corner = conn.shape
    tall = jnp.concatenate([conn, jnp.zeros((SUBS - cells, corner), jnp.int32)], axis=0)
    tall = jnp.transpose(tall.astype(F32))
    wanted = columns.astype(F32)
    return [jnp.where(tall[:, cell : cell + 1] == wanted, 1.0, 0.0).astype(BF16) for cell in range(cells)]


def first_kernel(plan, *refs):
    ins, refs = refs[:5], refs[5:]
    count = len(plan.lists) + 1
    outs, near_outs, refs = refs[:count], refs[count : 2 * count], refs[2 * count :]
    near_ins, spots_ref, match_ref, in_sems, out_sems = refs[:5], *refs[5:]
    fetches = [
        pltpu.make_async_copy(source, target, in_sems.at[place])
        for place, (source, target) in enumerate(zip(ins, near_ins))
    ]
    stores = [
        pltpu.make_async_copy(source, target, out_sems.at[place])
        for place, (source, target) in enumerate(zip(near_outs, outs))
    ]
    conn_ref, sides_ref, tops_ref, states_ref, mats_ref = near_ins
    send_refs, prods_ref = near_outs[: count - 1], near_outs[count - 1]
    for fetch in fetches:
        fetch.start()
    for fetch in fetches[:3]:
        fetch.wait()
    conn = conn_ref[...]
    for cell in range(conn.shape[0]):
        spots_ref[cell] = one_hot(conn[cell : cell + 1, :], spots_ref.shape[1])
    columns = face_slots(plan, sides_ref[...], tops_ref[...])
    for cell, match in enumerate(matches(conn, columns)):
        match_ref[cell] = match
    for fetch in fetches[3:]:
        fetch.wait()
    element_products(states_ref[...], mats_ref, spots_ref, prods_ref)
    stores[count - 1].start()
    send_faces(plan, prods_ref, match_ref, send_refs)
    for store in stores[: count - 1]:
        store.start()
    for store in stores:
        store.wait()


def first_part_kernel(
    plan, prods_ref, conn_ref, sides_ref, tops_ref, states_ref, index_ref, table_ref, *outs
):
    part_ref, shift_ref, spots_ref, match_ref, faces_ref = outs
    conn = conn_ref[...]
    for cell in range(conn.shape[0]):
        spots_ref[cell] = one_hot(conn[cell : cell + 1, :], spots_ref.shape[1])
    columns = face_slots(plan, sides_ref[...], tops_ref[...])
    for cell, match in enumerate(matches(conn, columns)):
        match_ref[cell] = match
    faces_ref[...] = one_hot(columns, faces_ref.shape[0])
    shift = shifted_potential(index_ref, table_ref)
    shift_ref[...] = shift
    part_ref[...] = over_cells(prods_ref, spots_ref, NT) + shift * states_ref[...].astype(F32)


def second_kernel(plan, part_ref, mats_ref, spots_ref, match_ref, faces_ref, *rest):
    count = len(plan.lists)
    recv_refs, send_refs = rest[:count], rest[count : 2 * count]
    first_ref, prods_ref, got_ref = rest[2 * count :]
    first = (part_ref[...] + got_faces(plan, recv_refs, faces_ref, got_ref)) / 3.0
    first_ref[...] = first
    element_products(first.astype(BF16), mats_ref, spots_ref, prods_ref)
    send_faces(plan, prods_ref, match_ref, send_refs)


def second_part_kernel(prods_ref, spots_ref, states_ref, first_ref, shift_ref, part_ref):
    applied = over_cells(prods_ref, spots_ref, NT) + shift_ref[...] * first_ref[...]
    part_ref[...] = 2.0 * applied / 3.0 - states_ref[...].astype(F32)


def third_kernel(plan, part_ref, faces_ref, *rest):
    count = len(plan.lists)
    recv_refs, (filtered_ref, mine_ref, other_ref, got_ref, gram_ref) = rest[:count], rest[count:]
    got = got_faces(plan, recv_refs, faces_ref, got_ref)
    filtered = (part_ref[...] + got * (2.0 / 3.0)).astype(BF16)
    filtered_ref[...] = filtered
    gram = mm(filtered, filtered, NT)
    third = gram.shape[0] // 3
    gram_ref[...] = gram[:, : 2 * third]
    gram_ref[:third, third:] = gram[2 * third :, 2 * third :]
    mine_ref[...] = gram_ref[half_rows(mine_ref, 0), :]
    other_ref[...] = gram_ref[half_rows(mine_ref, 1), :]


def half_rows(half_ref, other):
    half = half_ref.shape[0]
    core = lax.rem(lax.axis_index("gy"), 2)
    return pl.ds(pl.multiple_of((1 - core if other else core) * half, SUBS), half)


def invert_block(mat_ref, lead, lane0):
    tiles = BLOCK // SUBS
    shape = (SUBS, LANES)
    sub = lax.broadcasted_iota(jnp.int32, shape, 0)
    lane = lax.broadcasted_iota(jnp.int32, shape, 1)
    shift = lead - lane0

    def row(value, index):
        return jnp.broadcast_to(value[index : index + 1, :], shape)

    wide = min(LANES, mat_ref.shape[1] - lane0)
    rows = []
    for tile in range(tiles):
        loaded = mat_ref[lead + SUBS * tile : lead + SUBS * (tile + 1), lane0 : lane0 + wide]
        rows.append(loaded)
    cols = [
        [
            jnp.broadcast_to(rows[tile][:, shift + col : shift + col + 1], shape) if tile >= col // SUBS else None
            for tile in range(tiles)
        ]
        for col in range(BLOCK)
    ]
    inverse = [jnp.where(sub + (SUBS * tile + shift) == lane, 1.0, 0.0).astype(F32) for tile in range(tiles)]
    for col in range(BLOCK):
        own, at = divmod(col, SUBS)
        root = lax.rsqrt(row(cols[col][own], at))
        scaled = [cols[col][tile] * root if tile >= own else None for tile in range(tiles)]
        for later in range(col + 1, BLOCK):
            factor = row(scaled[later // SUBS], later % SUBS)
            for tile in range(later // SUBS, tiles):
                cols[later][tile] = cols[later][tile] - scaled[tile] * factor
        pivot_row = row(inverse[own], at) * root
        for tile in range(own, tiles):
            if tile == own:
                below = jnp.where(sub > at, scaled[tile], 0.0)
                inverse[tile] = jnp.where(sub == at, pivot_row, inverse[tile] - below * pivot_row)
            else:
                inverse[tile] = inverse[tile] - scaled[tile] * pivot_row
    return jnp.concatenate(inverse, axis=0)[:, :wide]


def rotate_kernel(total_slots, mine_ref, other_ref, filtered_ref, out_ref, packed_ref, mat_ref, acc_ref, inv_ref):
    width = mat_ref.shape[0]
    third = width // 3
    packed_ref[half_rows(mine_ref, 0), :] = mine_ref[...]
    packed_ref[half_rows(mine_ref, 1), :] = other_ref[...]
    packed = packed_ref[...] / total_slots
    mat_ref[:, : 2 * third] = packed
    mat_ref[: 2 * third, 2 * third :] = jnp.zeros((2 * third, third), F32)
    mat_ref[2 * third :, 2 * third :] = packed[:third, third:]
    full = (width, width)
    row = lax.broadcasted_iota(jnp.int32, full, 0)
    col = lax.broadcasted_iota(jnp.int32, full, 1)
    eye = row == col
    mat = mat_ref[...]
    diagonal = jnp.where(eye, mat, 0.0)
    scale_col = lax.rsqrt(jnp.sum(diagonal, axis=1, keepdims=True))
    scale_row = lax.rsqrt(jnp.sum(diagonal, axis=0, keepdims=True))
    mat_ref[...] = jnp.where(row >= col - col % BLOCK, mat * scale_col * scale_row, 0.0)
    acc_ref[...] = jnp.where(eye, 1.0, 0.0)
    for lead in range(0, width, BLOCK):
        lane0 = lead // LANES * LANES
        wide = min(LANES, width - lane0)
        block = invert_block(mat_ref, lead, lane0)
        rows_inv = mm32(block, acc_ref[lane0 : lane0 + wide, :])
        inv_ref[lead : lead + BLOCK, :] = (rows_inv * scale_row).astype(BF16)
        after = lead + BLOCK
        if after < width:
            lower = mm32(mat_ref[after:, lane0 : lane0 + wide], block, NT)
            whole = jnp.concatenate([jnp.zeros((after, BLOCK), F32), lower], axis=0)
            mat_ref[after:, :] = mat_ref[after:, :] - mm32(lower, whole, NT)
            acc_ref[after:, :] = acc_ref[after:, :] - mm32(lower, rows_inv)
    out_ref[...] = mm(inv_ref[...], filtered_ref[...]).astype(BF16)


def call(kernel, outs, scratch, *args, spaces=None, flops=0, moved=0):
    spaces = spaces or [pltpu.VMEM] * len(args)
    return pl.pallas_call(
        kernel,
        out_shape=outs,
        in_specs=[pl.BlockSpec(memory_space=space) for space in spaces],
        out_specs=jax.tree.map(lambda _: pl.BlockSpec(memory_space=pltpu.VMEM), outs),
        scratch_shapes=scratch,
        compiler_params=pltpu.CompilerParams(vmem_limit_bytes=VMEM),
        cost_estimate=pl.CostEstimate(flops=flops, bytes_accessed=moved, transcendentals=0),
    )(*args)


def pairs_of(size, phase):
    ups = [(i, i + 1) for i in range(phase, size - 1, 2)]
    return ups + [(j, i) for i, j in ups]


def sum_over_pairs(value, count, mate):
    if count & (count - 1):
        raise ValueError("device count")
    bits = [1 << place for place in range(count.bit_length() - 1) if 1 << place != mate]
    while bits:
        stage, bits = bits[:2], bits[2:]
        masks = stage + ([stage[0] | stage[1]] if len(stage) == 2 else [])
        got = [lax.ppermute(value, AXES, [(i, i ^ mask) for i in range(count)]) for mask in masks]
        value = value + got[0] if len(got) == 1 else (value + got[0]) + (got[1] + got[2])
    return value


def on_device(states, cell_matrices, connectivity, side_nodes, top_nodes, pot_index, pot_table):
    width, slots = states.shape
    cells, corner, _ = cell_matrices.shape
    sizes = [lax.axis_size(axis) for axis in AXES]
    plan = Plan(sizes, side_nodes.shape[1], top_nodes.shape[1])
    shape = jax.ShapeDtypeStruct
    field = shape((width, slots), F32)
    sends = [shape(plan.sent_shape(count, width), F32) for _, _, count, _ in plan.lists]
    prods_shape = shape((cells, 2 * width, corner), BF16)
    got = pltpu.VMEM((width, plan.total), F32)

    def swap(values):
        return [
            lax.ppermute(value, AXES[axis], pairs_of(sizes[axis], phase))
            for value, (axis, phase, _, _) in zip(values, plan.lists)
        ]

    spots_shape = shape((cells, slots, corner), BF16)
    match_shape = shape((cells, corner, plan.total), BF16)
    first_outs = [*sends, prods_shape]
    first_ins = (connectivity, side_nodes, top_nodes, states, cell_matrices)
    *sent, prods = pl.pallas_call(
        functools.partial(first_kernel, plan),
        out_shape=first_outs,
        in_specs=[pl.BlockSpec(memory_space=pltpu.HBM)] * len(first_ins),
        out_specs=[pl.BlockSpec(memory_space=pltpu.HBM)] * len(first_outs),
        scratch_shapes=[
            *[pltpu.VMEM(array.shape, array.dtype) for array in (*first_outs, *first_ins, spots_shape, match_shape)],
            pltpu.SemaphoreType.DMA((len(first_ins),)),
            pltpu.SemaphoreType.DMA((len(first_outs),)),
        ],
        compiler_params=pltpu.CompilerParams(vmem_limit_bytes=WHOLE_VMEM),
    )(*first_ins)
    got_first = swap(sent)
    scatter_flops = 4 * width * slots * cells * corner
    part, shift, spots, match, faces = call(
        functools.partial(first_part_kernel, plan),
        [
            field,
            shape((1, slots), F32),
            spots_shape,
            match_shape,
            shape((slots, plan.total), BF16),
        ],
        [],
        prods,
        connectivity,
        side_nodes,
        top_nodes,
        states,
        pot_index.reshape(1, slots),
        pot_table.reshape(1, -1),
        flops=scatter_flops,
    )
    *sent, first, prods = call(
        functools.partial(second_kernel, plan),
        [*sends, field, prods_shape],
        [got],
        part,
        cell_matrices,
        spots,
        match,
        faces,
        *got_first,
    )
    got_second = swap(sent)
    part = call(
        second_part_kernel, field, [], prods, spots, states, first, shift, flops=scatter_flops
    )
    third = width // 3
    half = shape((width // 2, 2 * third), F32)
    filtered, mine, other = call(
        functools.partial(third_kernel, plan),
        [shape((width, slots), BF16), half, half],
        [got, pltpu.VMEM((width, 2 * third), F32)],
        part,
        faces,
        *got_second,
    )
    mates = pairs_of(sizes[1], 0)
    mine = mine + lax.ppermute(other, "gy", mates)
    count = sizes[0] * sizes[1] * sizes[2]
    mine = sum_over_pairs(mine, count, sizes[2])
    other = lax.ppermute(mine, "gy", mates)
    square = pltpu.VMEM((width, width), F32)
    return call(
        functools.partial(rotate_kernel, slots * count),
        shape((width, slots), BF16),
        [pltpu.VMEM((width, 2 * third), F32), square, square, pltpu.VMEM((width, width), BF16)],
        mine,
        other,
        filtered,
    )


def solution(mesh):
    in_specs = (
        P(None, AXES),
        P(AXES, None, None),
        P(AXES, None),
        P(None, AXES),
        P(None, AXES),
        P(AXES),
        P(),
    )
    return jax.shard_map(
        on_device, mesh=mesh, in_specs=in_specs, out_specs=P(None, AXES), check_vma=False
    )
```

```python
import functools

import jax
import jax.numpy as jnp
from jax import lax
from jax.experimental import pallas as pl
from jax.experimental.pallas import tpu as pltpu
from jax.sharding import PartitionSpec as P

LANES = 128
SUBS = 8
BLOCK = 32
EARLY = 2
HEAD = 2
VMEM = 40 * 2**20
WHOLE_VMEM = 56 * 2**20
F32 = jnp.float32
BF16 = jnp.bfloat16
AXES = ("gx", "gy", "gz")
NN = (((1,), (0,)), ((), ()))
NT = (((1,), (1,)), ((), ()))


def mm(lhs, rhs, dims=NN):
    return lax.dot_general(lhs, rhs, dims, preferred_element_type=F32)


def mm32(lhs, rhs, dims=NN):
    return lax.dot_general(
        lhs, rhs, dims, precision=lax.Precision.HIGHEST, preferred_element_type=F32
    )


def split(value):
    high = value.astype(BF16)
    low = (value - high.astype(F32)).astype(BF16)
    return jnp.concatenate([high, low], axis=0)


def mm_split(value, rhs, dims=NN):
    both = mm(split(value), rhs, dims)
    rows = value.shape[0]
    return both[:rows] + both[rows:]


def padded(count):
    return -(-count // LANES) * LANES


class Plan:
    def __init__(self, mesh_sizes, side, top):
        self.sizes = mesh_sizes
        self.lists = []
        self.total = 0
        for axis, phase in ((1, 0), (1, 1), (0, 0), (0, 1), (2, 0), (2, 1)):
            if phase == 0 or mesh_sizes[axis] > 2:
                count = side if axis < 2 else top
                self.lists.append((axis, phase, count, self.total))
                self.total += padded(count)

        self.early, self.late = self.lists[:EARLY], self.lists[EARLY:]
        self.head, self.tail = self.lists[:HEAD], self.lists[HEAD:]

    def sent_shape(self, count, width):
        if 2 * count <= LANES and width % (2 * SUBS) == 0:
            return (width // 2, LANES)
        return (width, padded(count))


def columns_of(lists):
    return lists[0][3], lists[-1][3] + padded(lists[-1][2])


def one_hot(indices, rows):
    shape = (rows, indices.shape[1])
    return jnp.where(lax.broadcasted_iota(jnp.int32, shape, 0) == indices, 1.0, 0.0).astype(BF16)


def face_slots(plan, sides, tops):
    parts = []
    for axis, phase, count, _ in plan.lists:
        ref, row = (sides, 2 * axis) if axis < 2 else (tops, 0)
        lower, upper = ref[row : row + 1, :], ref[row + 1 : row + 2, :]
        place, size = lax.axis_index(AXES[axis]), plan.sizes[axis]
        below = lax.rem(place, 2) != phase
        paired = jnp.where(below, place > 0, place < size - 1)
        parts.append(jnp.where(paired, jnp.where(below, lower, upper), -1))
        if padded(count) > count:
            parts.append(jnp.full((1, padded(count) - count), -1, jnp.int32))
    return jnp.concatenate(parts, axis=1)


def shifted_potential(index_ref, table_ref):
    levels = table_ref.shape[1]
    picks = one_hot(index_ref[...], levels)
    table = table_ref[...]
    first = table.astype(BF16)
    rest = table - first.astype(F32)
    second = rest.astype(BF16)
    third = (rest - second.astype(F32)).astype(BF16)
    parts = mm(jnp.concatenate([first, second, third, first, first, first, first, first], 0), picks)
    return parts[0:1] + parts[1:2] + parts[2:3] - 0.5


def element_products(rounded, mats_ref, spots_ref, prods_ref):
    for cell in range(mats_ref.shape[0]):
        nodes = mm(rounded, spots_ref[cell]).astype(BF16)
        prods_ref[cell] = split(mm(nodes, mats_ref[cell]))


def joined(both):
    rows = both.shape[0] // 2
    return both[:rows] + both[rows:]


def over_cells(prods_ref, other_ref, dims, begin=0, end=None):
    total = None
    for cell in range(prods_ref.shape[0]):
        part = mm(prods_ref[cell], other_ref[cell, :, begin:end], dims)
        total = part if total is None else total + part
    return joined(total)


def send_faces(lists, prods_ref, match_ref, send_refs):
    begin, end = columns_of(lists)
    out = over_cells(prods_ref, match_ref, NN, begin, end)
    for (_, _, count, place), ref in zip(lists, send_refs):
        rows = ref.shape[0]
        place = place - begin
        if rows < out.shape[0]:
            ref[:, :count] = out[:rows, place : place + count]
            ref[:, LANES // 2 : LANES // 2 + count] = out[rows:, place : place + count]
        else:
            ref[...] = out[:, place : place + ref.shape[1]]


def got_faces(lists, recv_refs, faces_ref, got_ref):
    width = got_ref.shape[0]
    begin, end = columns_of(lists)
    for (_, _, count, place), ref in zip(lists, recv_refs):
        rows = ref.shape[0]
        wide = padded(count)
        place = place - begin
        if rows < width:
            got_ref[:, place : place + wide] = jnp.zeros((width, wide), F32)
            got_ref[:rows, place : place + count] = ref[:, :count]
            got_ref[rows:, place : place + count] = ref[:, LANES // 2 : LANES // 2 + count]
        else:
            got_ref[:, place : place + wide] = ref[...]
    return mm_split(got_ref[:, : end - begin], faces_ref[:, begin:end], NT)


def matches(conn, columns):
    cells, corner = conn.shape
    tall = jnp.concatenate([conn, jnp.zeros((SUBS - cells, corner), jnp.int32)], axis=0)
    tall = jnp.transpose(tall.astype(F32))
    wanted = columns.astype(F32)
    return [jnp.where(tall[:, cell : cell + 1] == wanted, 1.0, 0.0).astype(BF16) for cell in range(cells)]


def first_kernel(plan, *refs):
    ins, refs = refs[:5], refs[5:]
    count = len(plan.lists) + 1
    outs, near_outs, refs = refs[:count], refs[count : 2 * count], refs[2 * count :]
    near_ins, spots_ref, match_ref, in_sems, out_sems = refs[:5], *refs[5:]
    fetches = [
        pltpu.make_async_copy(source, target, in_sems.at[place])
        for place, (source, target) in enumerate(zip(ins, near_ins))
    ]
    stores = [
        pltpu.make_async_copy(source, target, out_sems.at[place])
        for place, (source, target) in enumerate(zip(near_outs, outs))
    ]
    conn_ref, sides_ref, tops_ref, states_ref, mats_ref = near_ins
    send_refs, prods_ref = near_outs[: count - 1], near_outs[count - 1]
    for fetch in fetches:
        fetch.start()
    for fetch in fetches[:3]:
        fetch.wait()
    conn = conn_ref[...]
    for cell in range(conn.shape[0]):
        spots_ref[cell] = one_hot(conn[cell : cell + 1, :], spots_ref.shape[1])
    columns = face_slots(plan, sides_ref[...], tops_ref[...])
    for cell, match in enumerate(matches(conn, columns)):
        match_ref[cell] = match
    for fetch in fetches[3:]:
        fetch.wait()
    element_products(states_ref[...], mats_ref, spots_ref, prods_ref)
    stores[count - 1].start()
    send_faces(plan.lists, prods_ref, match_ref, send_refs)
    for store in stores[: count - 1]:
        store.start()
    for store in stores:
        store.wait()


def first_part_kernel(
    plan, prods_ref, conn_ref, sides_ref, tops_ref, states_ref, index_ref, table_ref, *rest
):
    count = len(plan.early)
    recv_refs, (part_ref, shift_ref, spots_ref, match_ref, faces_ref, got_ref) = rest[:count], rest[count:]
    conn = conn_ref[...]
    for cell in range(conn.shape[0]):
        spots_ref[cell] = one_hot(conn[cell : cell + 1, :], spots_ref.shape[1])
    columns = face_slots(plan, sides_ref[...], tops_ref[...])
    for cell, match in enumerate(matches(conn, columns)):
        match_ref[cell] = match
    faces_ref[...] = one_hot(columns, faces_ref.shape[0])
    shift = shifted_potential(index_ref, table_ref)
    shift_ref[...] = shift
    own = over_cells(prods_ref, spots_ref, NT) + shift * states_ref[...].astype(F32)
    part_ref[...] = own + got_faces(plan.early, recv_refs, faces_ref, got_ref)


def second_kernel(plan, part_ref, mats_ref, spots_ref, match_ref, faces_ref, *rest):
    count = len(plan.late)
    recv_refs, rest = rest[:count], rest[count:]
    count = len(plan.head)
    send_refs, (first_ref, prods_ref, got_ref) = rest[:count], rest[count:]
    first = (part_ref[...] + got_faces(plan.late, recv_refs, faces_ref, got_ref)) / 3.0
    first_ref[...] = first
    element_products(first.astype(BF16), mats_ref, spots_ref, prods_ref)
    send_faces(plan.head, prods_ref, match_ref, send_refs)


def tail_faces_kernel(plan, prods_ref, match_ref, *send_refs):
    send_faces(plan.tail, prods_ref, match_ref, send_refs)


def second_part_kernel(plan, prods_ref, spots_ref, states_ref, first_ref, shift_ref, faces_ref, *rest):
    recv_refs, (part_ref, got_ref) = rest[: len(plan.early)], rest[len(plan.early) :]
    applied = over_cells(prods_ref, spots_ref, NT) + shift_ref[...] * first_ref[...]
    applied = applied + got_faces(plan.early, recv_refs, faces_ref, got_ref)
    part_ref[...] = 2.0 * applied / 3.0 - states_ref[...].astype(F32)


def third_kernel(plan, part_ref, faces_ref, *rest):
    count = len(plan.late)
    recv_refs, (filtered_ref, mine_ref, other_ref, got_ref, gram_ref) = rest[:count], rest[count:]
    got = got_faces(plan.late, recv_refs, faces_ref, got_ref)
    filtered = (part_ref[...] + got * (2.0 / 3.0)).astype(BF16)
    filtered_ref[...] = filtered
    gram = mm(filtered, filtered, NT)
    third = gram.shape[0] // 3
    gram_ref[...] = gram[:, : 2 * third]
    gram_ref[:third, third:] = gram[2 * third :, 2 * third :]
    mine_ref[...] = gram_ref[half_rows(mine_ref, 0), :]
    other_ref[...] = gram_ref[half_rows(mine_ref, 1), :]


def half_rows(half_ref, other):
    half = half_ref.shape[0]
    core = lax.rem(lax.axis_index("gy"), 2)
    return pl.ds(pl.multiple_of((1 - core if other else core) * half, SUBS), half)


def invert_block(rows, shift):
    tiles = BLOCK // SUBS
    wide = rows.shape[1]
    shape = (SUBS, wide)
    sub = lax.broadcasted_iota(jnp.int32, shape, 0)
    lane = lax.broadcasted_iota(jnp.int32, shape, 1)

    def row(value, index):
        return jnp.broadcast_to(value[index : index + 1, :], shape)

    def column(tile, col):
        return jnp.broadcast_to(rows[SUBS * tile : SUBS * (tile + 1), shift + col : shift + col + 1], shape)

    cols = [[column(tile, col) if tile >= col // SUBS else None for tile in range(tiles)] for col in range(BLOCK)]
    inverse = [jnp.where(sub + (SUBS * tile + shift) == lane, 1.0, 0.0).astype(F32) for tile in range(tiles)]
    for col in range(BLOCK):
        own, at = divmod(col, SUBS)
        root = lax.rsqrt(row(cols[col][own], at))
        scaled = [cols[col][tile] * root if tile >= own else None for tile in range(tiles)]
        for later in range(col + 1, BLOCK):
            factor = row(scaled[later // SUBS], later % SUBS)
            for tile in range(later // SUBS, tiles):
                cols[later][tile] = cols[later][tile] - scaled[tile] * factor
        pivot_row = row(inverse[own], at) * root
        for tile in range(own, tiles):
            if tile == own:
                below = jnp.where(sub > at, scaled[tile], 0.0)
                inverse[tile] = jnp.where(sub == at, pivot_row, inverse[tile] - below * pivot_row)
            else:
                inverse[tile] = inverse[tile] - scaled[tile] * pivot_row
    return jnp.concatenate(inverse, axis=0)


def rotate_kernel(
    total_slots, mine_ref, other_ref, filtered_ref, out_hbm, packed_ref, mat_ref, acc_ref, inv_ref, out_ref, sems
):
    width = mat_ref.shape[0]
    third = width // 3
    packed_ref[half_rows(mine_ref, 0), :] = mine_ref[...]
    packed_ref[half_rows(mine_ref, 1), :] = other_ref[...]
    packed = packed_ref[...] / total_slots
    mat_ref[:, : 2 * third] = packed
    mat_ref[: 2 * third, 2 * third :] = jnp.zeros((2 * third, third), F32)
    mat_ref[2 * third :, 2 * third :] = packed[:third, third:]
    full = (width, width)
    row = lax.broadcasted_iota(jnp.int32, full, 0)
    col = lax.broadcasted_iota(jnp.int32, full, 1)
    eye = row == col
    mat = mat_ref[...]
    diagonal = jnp.where(eye, mat, 0.0)
    scale_col = lax.rsqrt(jnp.sum(diagonal, axis=1, keepdims=True))
    scale_row = lax.rsqrt(jnp.sum(diagonal, axis=0, keepdims=True))
    mat_ref[...] = jnp.where(row >= col - col % BLOCK, mat * scale_col * scale_row, 0.0)
    acc_ref[...] = jnp.where(eye, 1.0, 0.0)
    leads = list(range(0, width, BLOCK))
    early = width - width % LANES if width > LANES else 0
    stores = []

    def tile_of(lead):
        lane0 = lead // LANES * LANES
        return lane0, min(lane0 + LANES, width)

    def rotate(begin, end):
        out_ref[begin:end, :] = mm(inv_ref[begin:end, :], filtered_ref[...]).astype(BF16)
        stores.append(
            pltpu.make_async_copy(out_ref.at[begin:end], out_hbm.at[begin:end], sems.at[len(stores)])
        )
        stores[-1].start()

    def later(lead, block, head):
        begin, end = tile_of(lead)
        after = lead + BLOCK
        rows_inv = mm32(block, acc_ref[begin:end, :])
        inv_ref[lead:after, :] = (rows_inv * scale_row).astype(BF16)
        if after == width:
            return
        acc_ref[after : after + BLOCK, :] = acc_ref[after : after + BLOCK, :] - mm32(head, rows_inv)
        beyond = after + BLOCK
        if beyond == width:
            return
        lower = mm32(mat_ref[beyond:, begin:end], block, NT)
        acc_ref[beyond:, :] = acc_ref[beyond:, :] - mm32(lower, rows_inv)
        whole = jnp.concatenate([jnp.zeros((after, BLOCK), F32), head, lower], axis=0)
        mat_ref[beyond:, :] = mat_ref[beyond:, :] - mm32(lower, whole, NT)

    begin, end = tile_of(0)
    diag = mat_ref[:BLOCK, begin:end]
    waiting = None
    for lead in leads:
        begin, end = tile_of(lead)
        block = invert_block(diag, lead - begin)
        if waiting is not None:
            later(*waiting)
        if early and lead == early:
            rotate(0, early)
        after = lead + BLOCK
        head = None
        if after < width:
            head = mm32(mat_ref[after : after + BLOCK, begin:end], block, NT)
            first, last = tile_of(after)
            parts = [head]
            if after > first:
                parts.insert(0, jnp.zeros((after - first, BLOCK), F32))
            if last > after + BLOCK:
                parts.append(jnp.zeros((last - after - BLOCK, BLOCK), F32))
            tall = jnp.concatenate(parts, axis=0) if len(parts) > 1 else head
            diag = mat_ref[after : after + BLOCK, first:last] - mm32(head, tall, NT)
        waiting = (lead, block, head)
    later(*waiting)
    rotate(early, width)
    for store in stores:
        store.wait()


def call(kernel, outs, scratch, *args, spaces=None, flops=0, moved=0):
    spaces = spaces or [pltpu.VMEM] * len(args)
    return pl.pallas_call(
        kernel,
        out_shape=outs,
        in_specs=[pl.BlockSpec(memory_space=space) for space in spaces],
        out_specs=jax.tree.map(lambda _: pl.BlockSpec(memory_space=pltpu.VMEM), outs),
        scratch_shapes=scratch,
        compiler_params=pltpu.CompilerParams(vmem_limit_bytes=VMEM),
        cost_estimate=pl.CostEstimate(flops=flops, bytes_accessed=moved, transcendentals=0),
    )(*args)


def pairs_of(size, phase):
    ups = [(i, i + 1) for i in range(phase, size - 1, 2)]
    return ups + [(j, i) for i, j in ups]


def swap_pairs(sizes, axis, phase):
    strides = (sizes[1] * sizes[2], sizes[2], 1)
    other = 2 if axis == 1 else 1
    pairs = []
    for number in range(sizes[0] * strides[0]):
        place = [number // stride % size for stride, size in zip(strides, sizes)]
        step = 1 if place[axis] % 2 == phase else -1
        if 0 <= place[axis] + step < sizes[axis]:
            pairs.append((number, number + step * strides[axis]))
        elif sizes[other] % 2 == 0:
            pairs.append((number, number + (1 - 2 * (place[other] % 2)) * strides[other]))
    return pairs


def sum_over_pairs(value, count, mate):
    if count & (count - 1):
        raise ValueError("device count")
    bits = [1 << place for place in range(count.bit_length() - 1) if 1 << place != mate]
    while bits:
        stage, bits = bits[:2], bits[2:]
        masks = stage + ([stage[0] | stage[1]] if len(stage) == 2 else [])
        got = [lax.ppermute(value, AXES, [(i, i ^ mask) for i in range(count)]) for mask in masks]
        value = value + got[0] if len(got) == 1 else (value + got[0]) + (got[1] + got[2])
    return value


def on_device(states, cell_matrices, connectivity, side_nodes, top_nodes, pot_index, pot_table):
    width, slots = states.shape
    cells, corner, _ = cell_matrices.shape
    sizes = [lax.axis_size(axis) for axis in AXES]
    plan = Plan(sizes, side_nodes.shape[1], top_nodes.shape[1])
    shape = jax.ShapeDtypeStruct
    field = shape((width, slots), F32)
    sends = [shape(plan.sent_shape(count, width), F32) for _, _, count, _ in plan.lists]
    prods_shape = shape((cells, 2 * width, corner), BF16)
    early = len(plan.early)
    got_early, got_late = [
        pltpu.VMEM((width, columns_of(lists)[1] - columns_of(lists)[0]), F32) for lists in (plan.early, plan.late)
    ]

    def swap(values, lists):
        return [
            lax.ppermute(value, AXES, swap_pairs(sizes, axis, phase))
            for value, (axis, phase, _, _) in zip(values, lists)
        ]

    spots_shape = shape((cells, slots, corner), BF16)
    match_shape = shape((cells, corner, plan.total), BF16)
    first_outs = [*sends, prods_shape]
    first_ins = (connectivity, side_nodes, top_nodes, states, cell_matrices)
    *sent, prods = pl.pallas_call(
        functools.partial(first_kernel, plan),
        out_shape=first_outs,
        in_specs=[pl.BlockSpec(memory_space=pltpu.HBM)] * len(first_ins),
        out_specs=[pl.BlockSpec(memory_space=pltpu.HBM)] * len(first_outs),
        scratch_shapes=[
            *[pltpu.VMEM(array.shape, array.dtype) for array in (*first_outs, *first_ins, spots_shape, match_shape)],
            pltpu.SemaphoreType.DMA((len(first_ins),)),
            pltpu.SemaphoreType.DMA((len(first_outs),)),
        ],
        compiler_params=pltpu.CompilerParams(vmem_limit_bytes=WHOLE_VMEM),
    )(*first_ins)
    got_first = swap(sent, plan.lists)
    scatter_flops = 4 * width * slots * cells * corner
    part, shift, spots, match, faces = call(
        functools.partial(first_part_kernel, plan),
        [
            field,
            shape((1, slots), F32),
            spots_shape,
            match_shape,
            shape((slots, plan.total), BF16),
        ],
        [got_early],
        prods,
        connectivity,
        side_nodes,
        top_nodes,
        states,
        pot_index.reshape(1, slots),
        pot_table.reshape(1, -1),
        *got_first[:early],
        flops=scatter_flops,
    )
    *sent, first, prods = call(
        functools.partial(second_kernel, plan),
        [*sends[:HEAD], field, prods_shape],
        [got_late],
        part,
        cell_matrices,
        spots,
        match,
        faces,
        *got_first[early:],
    )
    got_second = swap(sent, plan.head)
    if plan.tail:
        sent = call(functools.partial(tail_faces_kernel, plan), sends[HEAD:], [], prods, match)
        got_second += swap(sent, plan.tail)
    part = call(
        functools.partial(second_part_kernel, plan),
        field,
        [got_early],
        prods,
        spots,
        states,
        first,
        shift,
        faces,
        *got_second[:early],
        flops=scatter_flops,
    )
    third = width // 3
    half = shape((width // 2, 2 * third), F32)
    filtered, mine, other = call(
        functools.partial(third_kernel, plan),
        [shape((width, slots), BF16), half, half],
        [got_late, pltpu.VMEM((width, 2 * third), F32)],
        part,
        faces,
        *got_second[early:],
    )
    mates = pairs_of(sizes[1], 0)
    mine = mine + lax.ppermute(other, "gy", mates)
    count = sizes[0] * sizes[1] * sizes[2]
    mine = sum_over_pairs(mine, count, sizes[2])
    other = lax.ppermute(mine, "gy", mates)
    square = pltpu.VMEM((width, width), F32)
    vmem = pl.BlockSpec(memory_space=pltpu.VMEM)
    return pl.pallas_call(
        functools.partial(rotate_kernel, slots * count),
        out_shape=shape((width, slots), BF16),
        in_specs=[vmem] * 3,
        out_specs=pl.BlockSpec(memory_space=pltpu.HBM),
        scratch_shapes=[
            pltpu.VMEM((width, 2 * third), F32),
            square,
            square,
            pltpu.VMEM((width, width), BF16),
            pltpu.VMEM((width, slots), BF16),
            pltpu.SemaphoreType.DMA((2,)),
        ],
        compiler_params=pltpu.CompilerParams(vmem_limit_bytes=VMEM),
    )(mine, other, filtered)


def solution(mesh):
    in_specs = (
        P(None, AXES),
        P(AXES, None, None),
        P(AXES, None),
        P(None, AXES),
        P(None, AXES),
        P(AXES),
        P(),
    )
    return jax.shard_map(
        on_device, mesh=mesh, in_specs=in_specs, out_specs=P(None, AXES), check_vma=False
    )
```
